32 devices in a mesh: groups: 2 (over y), task: 4 (over x, core), tensor: 4 (over z).
Axes of the slice: x: 2, y: 2, z: 4, core: 2. Of those that a mesh axis runs over, the one named last changes fastest.
Arguments:
- attention: bfloat16 [4096, 8192], P(('groups', 'task'), 'tensor'), parts along dimension 0, may hold values from -6 to 6
- out_weight: bfloat16 [8192, 5120], P('tensor'), may hold values from -0.09375 to 0.09375
- task_tags: int32 [4096], P(('groups', 'task')), parts along dimension 0, may hold values from 0 to 63, as said below
- delta_values: bfloat16 [64, 8, 128, 128], P('task', 'tensor'), may hold values from -0.5 to 0.5
- block_rows: int32 [64, 8], P('task', 'tensor'), may hold values from 0 to 15
- block_columns: int32 [64, 8], P('task', 'tensor'), may hold values from 0 to 39
- block_live: int32 [64, 8], P('task', 'tensor'), may hold values 0 or 1
Outputs:
- projected: bfloat16 [4096, 5120], P(('groups', 'task'), 'tensor'), parts along dimension 0
The draws below stay inside these ranges and needn't reach their ends.
There are 2 independent parts, one for each index of `groups`. The reference program is written for one: setup_inputs(seed, part) draws one part's arguments, and reference() takes and returns one part's arrays. A program takes and returns all parts, laid end to end along the dimension named above; an argument that names none is the same for every part. Nothing has to cross between parts.
Inputs may be any that keep to these rules, and one draw needn't show every extreme that they name: `task_tags`: the tasks form owner groups of 64 / (size of axis task) consecutive tasks. Each device's 512 rows name tasks of any one owner group at most 192 times, and one owner group, the same for every device's rows, exactly 192 times.
All inputs are finite; a program needn't handle non-finite values. No bound on the sum of `block_live` on one device may be relied on, other than what follows from the above.
Results may differ from the reference program's by a relative error of at most 0.001.
Values may be sent and summed in bfloat16 or wider, within the bound.
A program may use at most 128 MiB of HBM per device.

```python
import jax
import jax.numpy as jnp
from jax import lax

D = 5120
HEADS = 64
HD = 128
TASKS = 64
KSLOT = 2
R_DEV = 512
ROWS = 2048
SLOTS = 8
CAP = 192
N_TASK = 4
N_TENSOR = 4


def draw_task_tags(key, part):
    key = jax.random.fold_in(key, 7)
    hot_key, rotate_key, task_key, order_key = jax.random.split(key, 4)
    per_owner = TASKS // N_TASK
    hot_owner = jax.random.randint(hot_key, (), 0, N_TASK)
    position = jnp.arange(R_DEV)
    rotation = jax.random.randint(rotate_key, (N_TASK, 1), 0, N_TASK - 1)
    others = (position[None, :] - CAP + rotation) % (N_TASK - 1)
    others = others + (others >= hot_owner).astype(others.dtype)
    owner_ids = jnp.where(position[None, :] < CAP, hot_owner, others)
    ordering = jax.vmap(lambda sub_key: jax.random.permutation(sub_key, R_DEV))(jax.random.split(order_key, N_TASK))
    owner_ids = jnp.take_along_axis(owner_ids, ordering, axis=1)
    within = jax.random.randint(task_key, (N_TASK, R_DEV), 0, per_owner)
    return (owner_ids * per_owner + within).reshape(-1).astype(jnp.int32)


def with_ends(drawn, own_key, smallest, top_value):
    longest = drawn.shape.index(max(drawn.shape))
    spots = []
    for shift in (0, 1):
        where = [jax.random.randint(jax.random.fold_in(own_key, axis), (), 0, length) for axis, length in enumerate(drawn.shape)]
        where[longest] = (where[longest] + shift) % drawn.shape[longest]
        spots.append(tuple(where))
    return drawn.at[spots[0]].set(smallest).at[spots[1]].set(top_value)


def raised(result, stream_key, source, target, parts, factor):
    owner, partner = [(jnp.arange(result.shape[dim]) // (result.shape[dim] // parts)).reshape([-1 if axis == dim else 1 for axis in range(result.ndim)]) for dim in (source, target)]
    chosen = jax.random.permutation(stream_key, parts)[partner]
    strong = (owner == chosen) | (owner == (partner + parts // 2) % parts)
    return jnp.where(strong, factor * result, result)


def levels(key, dims, cuts, smallest, largest):
    level = 1.0
    for axis_at, shards_of in cuts:
        steps = jax.random.uniform(jax.random.fold_in(jax.random.fold_in(key, 6), axis_at), (shards_of,), jnp.float32, smallest / len(cuts), largest / len(cuts))
        level = level * jnp.repeat(jnp.exp(steps), dims[axis_at] // shards_of).reshape((-1,) + (1,) * (len(dims) - 1 - axis_at))
    return level


def gaussian(rng, extent, scale, reach, shards=(), kind=jnp.bfloat16):
    drawn = scale * jax.random.normal(rng, extent, jnp.float32)
    if shards:
        drawn = drawn * levels(rng, extent, shards, -0.22, 0.18)
    return jnp.clip(drawn, -reach, reach).astype(kind)


def bell_draw_with(own_key, dims, width, most, pieces, heavy, kind=jnp.bfloat16):
    result = width * jax.random.normal(own_key, dims, jnp.float32)
    if pieces:
        result = result * levels(own_key, dims, pieces, -0.22, 0.18)
    return jnp.clip(raised(result, jax.random.fold_in(own_key, 3), *heavy), -most, most).astype(kind)


def setup_inputs(seed: int = 0, part: int = 0) -> dict:
    key_list = jax.random.split(jax.random.key(seed), 8)
    part_splits = jax.random.split(jax.random.fold_in(key_list[7], part), 8)
    return {
        "attention": gaussian(part_splits[0], (ROWS, HEADS * HD), 1.0, 6.0, ((0, 4), (1, 4))),
        "out_weight": bell_draw_with(key_list[1], (HEADS * HD, D), (HEADS * HD) ** -0.5, 0.09375, ((0, 4),), (0, 1, 4, 2.0)),
        "task_tags": draw_task_tags(jax.random.fold_in(jax.random.fold_in(key_list[7], part), 71), part),
        "delta_values": gaussian(key_list[3], (TASKS, SLOTS, HD, HD), HD ** -0.5, 0.5, ((0, 4), (1, 4))),
        "block_rows": with_ends(jax.random.randint(key_list[4], (TASKS, SLOTS), 0, HEADS // N_TENSOR), jax.random.fold_in(key_list[4], 1), 0, (HEADS // N_TENSOR) - 1).astype(jnp.int32),
        "block_columns": with_ends(jax.random.randint(key_list[5], (TASKS, SLOTS), 0, D // HD), jax.random.fold_in(key_list[5], 1), 0, (D // HD) - 1).astype(jnp.int32),
        "block_live": with_ends((jax.random.randint(key_list[6], (TASKS, SLOTS), 0, 4) < 3).astype(jnp.int32), jax.random.fold_in(key_list[6], 1), 0, 1),
    }


def reference(attention, out_weight, task_tags, delta_values, block_rows, block_columns, block_live):
    base_sum = jnp.dot(attention, out_weight, preferred_element_type=jnp.float32)
    rows_count = attention.shape[0]
    heads_all = attention.reshape(rows_count, HEADS, HD)
    per_shard = HEADS // N_TENSOR
    col_blocks = D // HD
    row_ids = jnp.arange(rows_count)
    block_ids = jnp.arange(col_blocks)

    def one_slot(slot_index, total):
        matrices = lax.dynamic_index_in_dim(delta_values, slot_index, 1, keepdims=False)[task_tags]
        rows_pick = lax.dynamic_index_in_dim(block_rows, slot_index, 1, keepdims=False)[task_tags]
        cols_pick = lax.dynamic_index_in_dim(block_columns, slot_index, 1, keepdims=False)[task_tags]
        live_pick = lax.dynamic_index_in_dim(block_live, slot_index, 1, keepdims=False)[task_tags]
        head_index = (slot_index // KSLOT) * per_shard + rows_pick
        chosen = heads_all[row_ids, head_index]
        product = jnp.einsum('rd,rde->re', chosen.astype(jnp.float32), matrices.astype(jnp.float32))
        product = product * live_pick.astype(jnp.float32)[:, None]
        placing = (cols_pick[:, None] == block_ids[None, :]).astype(jnp.float32)
        return total + (placing[:, :, None] * product[:, None, :]).reshape(rows_count, D)

    total = lax.fori_loop(0, SLOTS, one_slot, base_sum)
    return total.astype(jnp.bfloat16)
```

```python
import functools

import jax
import jax.numpy as jnp
from jax import lax
from jax.experimental import pallas as pl
from jax.experimental.pallas import tpu as pltpu
from jax.sharding import PartitionSpec as P


def pick(lookup, onehot):
    return jnp.sum(onehot * lookup, axis=-1)


def select_head(shard_heads, head_index):
    head_hits = (head_index[..., None] == jnp.arange(shard_heads.shape[-2])).astype(jnp.bfloat16)
    return jnp.einsum(
        "...hd,...h->...d", shard_heads, head_hits, preferred_element_type=jnp.float32
    ).astype(jnp.bfloat16)


def local_general(attention, out_weight, task_tags, delta_values, block_rows, block_columns, block_live):
    rows_count = attention.shape[0]
    width = out_weight.shape[1]
    head_dim = delta_values.shape[-1]
    per_shard = attention.shape[1] // head_dim
    owned_tasks = delta_values.shape[0]
    slot_count = delta_values.shape[1]
    col_blocks = width // head_dim
    owners = lax.axis_size("task")
    capacity = rows_count * 3 // 8
    owner_ids = task_tags // owned_tasks
    member = (owner_ids[:, None] == jnp.arange(owners)[None, :]).astype(jnp.int32)
    bucket_rank = jnp.sum(jnp.cumsum(member, axis=0) * member, axis=1) - 1
    placing = owner_ids * capacity + bucket_rank
    slot_tasks = (
        jnp.full((owners * capacity,), -1, jnp.int32)
        .at[placing]
        .set(task_tags - owner_ids * owned_tasks)
        .reshape(owners, capacity)
    )
    sending = (
        jnp.zeros((owners * capacity, attention.shape[1]), jnp.bfloat16).at[placing].set(attention)
    )
    sending = sending.reshape(owners, capacity, attention.shape[1])
    rows_in = lax.all_to_all(sending, "task", split_axis=0, concat_axis=0, tiled=True)
    task_ids = lax.all_to_all(slot_tasks, "task", split_axis=0, concat_axis=0, tiled=True)
    member_own = (task_ids[..., None] == jnp.arange(owned_tasks)).astype(jnp.int32)
    member_bf = member_own.astype(jnp.bfloat16)
    heads_in = rows_in.reshape(rows_in.shape[0], rows_in.shape[1], per_shard, head_dim)
    results = []
    found = []
    for slot_index in range(slot_count):
        chosen = select_head(heads_in, pick(block_rows[:, slot_index], member_own))
        spread = chosen[:, :, None, :] * member_bf[..., None]
        product = jnp.einsum(
            "abtd,tde->abe", spread, delta_values[:, slot_index], preferred_element_type=jnp.float32
        )
        results.append(
            product * pick(block_live[:, slot_index], member_own).astype(jnp.float32)[..., None]
        )
        found.append(pick(block_columns[:, slot_index], member_own))
    values_back = lax.all_to_all(
        jnp.stack(results, axis=2), "task", split_axis=0, concat_axis=0, tiled=True
    )
    columns_back = lax.all_to_all(
        jnp.stack(found, axis=2), "task", split_axis=0, concat_axis=0, tiled=True
    )
    values = values_back.reshape(owners * capacity, slot_count, head_dim)[placing]
    columns = columns_back.reshape(owners * capacity, slot_count)[placing]
    column_hits = (columns[:, :, None] == jnp.arange(col_blocks)).astype(jnp.float32)
    placed_delta = jnp.einsum(
        "rkc,rkd->cdr", column_hits, values, precision=lax.Precision.HIGHEST
    ).reshape(width, rows_count)
    base_part = lax.dot_general(
        out_weight, attention, (((0,), (1,)), ((), ())), preferred_element_type=jnp.float32
    )
    summed = lax.psum_scatter(base_part + placed_delta, "tensor", scatter_dimension=0, tiled=True)
    return summed.T.astype(jnp.bfloat16)


MESH = pl.DeviceIdType.MESH
PIECES = 4
RING = 4
WIDE = 256
LEVELS = 32766.0


def fits(mesh):
    shards = mesh.shape["tensor"]
    return 5120 % (shards * 256) == 0 and mesh.shape["groups"] == 2 and mesh.shape["task"] % 2 == 0


def kernel(
    n, owners, att_ref, w_ref, tag_ref, tab_ref, delta_ref, out_ref,
    part, wbuf, tab_all, onehot_info, chosen, vals, dbuf, spread,
    fsend, fscale, frecv, frscale, bsend, bscale, brecv, brscale,
    wsem, tab_ssem, tab_rsem, own_ssem, own_rsem,
    x_ssem, x_rsem, y_ssem, y_rsem, c_ssem, c_rsem,
    f_ssem, f_rsem, fs_ssem, fs_rsem, b_ssem, b_rsem, bs_ssem, bs_rsem,
):
    rows = att_ref.shape[0]
    blocks = part.shape[0]
    per = blocks // n
    g = lax.axis_index("groups")
    t = lax.axis_index("task")
    z = lax.axis_index("tensor")
    twin = t + 1 - 2 * lax.rem(t, 2)
    hops = range(2, owners, 2)
    owned = tab_ref.shape[0]
    steps = blocks * 128 // WIDE

    def wcopy(i):
        slot = lax.rem(i, RING)
        return pltpu.make_async_copy(
            w_ref.at[:, pl.ds(pl.multiple_of(i * WIDE, WIDE), WIDE)], wbuf.at[slot], wsem.at[slot]
        )

    for i in range(RING - 1):
        wcopy(i).start()

    barrier = pltpu.get_barrier_semaphore()
    for k in range(1, owners):
        pl.semaphore_signal(barrier, 1, device_id={"task": lax.rem(t + k, owners)}, device_id_type=MESH)
    pl.semaphore_signal(barrier, 1, device_id={"groups": 1 - g}, device_id_type=MESH)

    @pl.when(z > 0)
    def _():
        pl.semaphore_signal(barrier, 1, device_id={"tensor": z - 1}, device_id_type=MESH)

    @pl.when(z < n - 1)
    def _():
        pl.semaphore_signal(barrier, 1, device_id={"tensor": z + 1}, device_id_type=MESH)

    pl.semaphore_wait(barrier, owners + (z + n - 1) // n + (2 * n - 2 - z) // n)

    def remote(src, dst, ssem, rsem, where):
        return pltpu.make_async_remote_copy(
            src_ref=src, dst_ref=dst, send_sem=ssem, recv_sem=rsem, device_id=where, device_id_type=MESH
        )

    def tab_copy(k):
        here = tab_all.at[pl.ds(pl.multiple_of(t * owned, owned), owned)]
        return remote(tab_ref, here, tab_ssem.at[k], tab_rsem.at[k], {"task": lax.rem(t + k, owners)})

    def x_copy(h, q):
        return remote(
            delta_ref.at[g, q], dbuf.at[t, g, q], x_ssem.at[h, q], x_rsem.at[h, q],
            {"task": lax.rem(t + 2 * h + 2, owners)},
        )

    def y_copy(h, q):
        src = lax.rem(t - 2 * h - 2 + owners, owners)
        return remote(
            dbuf.at[src, g, q], dbuf.at[src, g, q], y_ssem.at[h, q], y_rsem.at[h, q], {"groups": 1 - g}
        )

    def c_copy(h, q, half):
        src = lax.rem(t - 2 * h - 2 + owners, owners)
        slot = g if half == 0 else 1 - g
        return remote(
            dbuf.at[src, slot, q], dbuf.at[src, slot, q], c_ssem.at[half, h, q], c_rsem.at[half, h, q],
            {"task": twin},
        )

    own_copy = remote(delta_ref, dbuf.at[t], own_ssem, own_rsem, {"task": twin})
    for k in range(1, owners):
        tab_copy(k).start()
    for q in range(PIECES):
        for h in range(len(hops)):
            x_copy(h, q).start()
    own_copy.start()
    tab_all[pl.ds(pl.multiple_of(t * owned, owned), owned), :] = tab_ref[...]

    def base_step(i, carry):
        @pl.when(i + RING - 1 < steps)
        def _():
            wcopy(i + RING - 1).start()

        wcopy(i).wait()
        got = jnp.dot(att_ref[...], wbuf[lax.rem(i, RING)], preferred_element_type=jnp.float32)
        for e in range(WIDE // 128):
            part[i * (WIDE // 128) + e] = got[:, e * 128 : (e + 1) * 128]
        return carry

    for q in range(PIECES):
        lax.fori_loop(steps * q // PIECES, steps * (q + 1) // PIECES, base_step, 0)
        for h in range(len(hops)):
            x_copy(h, q).wait_recv()
            y_copy(h, q).start()
            c_copy(h, q, 0).start()

    for k in range(1, owners):
        tab_copy(k).wait_recv()
    tasks = tab_all.shape[0]
    hits = tag_ref[:, :tasks] == lax.broadcasted_iota(jnp.int32, (rows, tasks), 1)
    onehot = jnp.where(hits, 1.0, 0.0).astype(jnp.bfloat16)
    onehot_info[...] = jnp.dot(onehot, tab_all[...], preferred_element_type=jnp.float32)
    tile = 64

    def choose(i, carry):
        at = pl.ds(pl.multiple_of(i * tile, tile), tile)
        heads = [onehot_info[at, s * 128 : (s + 1) * 128] for s in range(2)]
        picked = [jnp.zeros((tile, 128), jnp.float32) for s in range(2)]
        for h in range(att_ref.shape[1] // 128):
            block = att_ref[at, h * 128 : (h + 1) * 128].astype(jnp.float32)
            for s in range(2):
                picked[s] = jnp.where(heads[s] == float(h), block, picked[s])
        for s in range(2):
            chosen[s, at, :] = picked[s]
        return carry

    lax.fori_loop(0, rows // tile, choose, 0)
    vals[...] = jnp.zeros_like(vals)

    def add_piece(source, owner, s, q):
        each = owned // PIECES
        for e in range(each):
            task = owner * owned + q * each + e
            spread[:, e * 128 : (e + 1) * 128] = jnp.where(
                tag_ref[...] == task, chosen[s], 0.0
            ).astype(jnp.bfloat16)
        vals[s] += jnp.dot(spread[...], source, preferred_element_type=jnp.float32)

    def add_half(ref, owner, s):
        def body(q, carry):
            add_piece(ref[s, q], owner, s, q)
            return carry

        lax.fori_loop(0, PIECES, body, 0)

    for s in range(2):
        add_half(delta_ref, t, s)
    own_copy.wait_recv()
    for s in range(2):
        add_half(dbuf.at[twin], twin, s)
    for h in range(len(hops)):
        src = lax.rem(t - 2 * h - 2 + owners, owners)
        add_half(dbuf.at[src], src, g)
    for q in range(PIECES):
        for h in range(len(hops)):
            y_copy(h, q).wait_recv()
            c_copy(h, q, 1).start()
    for h in range(len(hops)):
        src = lax.rem(t - 2 * h - 2 + owners, owners)
        add_half(dbuf.at[src], src, 1 - g)
        other = lax.rem(twin - 2 * h - 2 + owners, owners)
        for q in range(PIECES):
            c_copy(h, q, 0).wait_recv()
            c_copy(h, q, 1).wait_recv()
        for s in range(2):
            add_half(dbuf.at[other], other, s)
    for s in range(2):
        vals[s] = vals[s] * onehot_info[:, (4 + s) * 128 : (5 + s) * 128]

    def block_sum(c):
        total = part[c]
        for s in range(2):
            mine = onehot_info[:, (2 + s) * 128 : (3 + s) * 128] == c.astype(jnp.float32)
            total = total + jnp.where(mine, vals[s], 0.0)
        return total

    def decoded(ref, scales, i):
        whole = ref[i].astype(jnp.int32).astype(jnp.float32).reshape(rows // 8, 8, 128)
        return (whole * scales[i][None]).reshape(rows, 128)

    def encode(total, ref, scales, i):
        cut = total.reshape(rows // 8, 8, 128)
        top = jnp.maximum(jnp.max(jnp.abs(cut), axis=0), 1e-30)
        scales[i] = top * (1.0 / LEVELS)
        levels = jnp.round(cut * (LEVELS / top)[None]).reshape(rows, 128)
        ref[i] = levels.astype(jnp.int32).astype(jnp.int16)

    def f_copies(i):
        where = {"tensor": z + 1}
        return (
            remote(fsend.at[i], frecv.at[i], f_ssem.at[i], f_rsem.at[i], where),
            remote(fscale.at[i], frscale.at[i], fs_ssem.at[i], fs_rsem.at[i], where),
        )

    def b_copies(i):
        where = {"tensor": z - 1}
        return (
            remote(bsend.at[i], brecv.at[i], b_ssem.at[i], b_rsem.at[i], where),
            remote(bscale.at[i], brscale.at[i], bs_ssem.at[i], bs_rsem.at[i], where),
        )

    f_count = (n - 1 - z) * per
    b_count = z * per

    def chain(i, carry):
        @pl.when(i < f_count)
        def _():
            part_at = (n - 1 - i // per) * per + i % per

            @pl.when(z == 0)
            def _():
                encode(block_sum(part_at), fsend, fscale, i)

            @pl.when(z > 0)
            def _():
                for copy in f_copies(i):
                    copy.wait_recv()
                encode(block_sum(part_at) + decoded(frecv, frscale, i), fsend, fscale, i)

            for copy in f_copies(i):
                copy.start()

        @pl.when(i < b_count)
        def _():
            @pl.when(z == n - 1)
            def _():
                encode(block_sum(i), bsend, bscale, i)

            @pl.when(z < n - 1)
            def _():
                for copy in b_copies(i):
                    copy.wait_recv()
                encode(block_sum(i) + decoded(brecv, brscale, i), bsend, bscale, i)

            for copy in b_copies(i):
                copy.start()

        return carry

    lax.fori_loop(0, (n - 1) * per, chain, 0)

    def finish(j, carry):
        part[z * per + j] = block_sum(z * per + j)

        @pl.when(z < n - 1)
        def _():
            i = z * per + j
            for copy in b_copies(i):
                copy.wait_recv()
            part[z * per + j] += decoded(brecv, brscale, i)

        @pl.when(z > 0)
        def _():
            i = (n - 1 - z) * per + j
            for copy in f_copies(i):
                copy.wait_recv()
            part[z * per + j] += decoded(frecv, frscale, i)

        out_ref[:, pl.ds(pl.multiple_of(j * 128, 128), 128)] = part[z * per + j].astype(out_ref.dtype)
        return carry

    lax.fori_loop(0, per, finish, 0)

    def drain(i, carry):
        @pl.when(i < f_count)
        def _():
            for copy in f_copies(i):
                copy.wait_send()

        @pl.when(i < b_count)
        def _():
            for copy in b_copies(i):
                copy.wait_send()

        return carry

    lax.fori_loop(0, (n - 1) * per, drain, 0)
    for k in range(1, owners):
        tab_copy(k).wait_send()
    own_copy.wait_send()
    for q in range(PIECES):
        for h in range(len(hops)):
            x_copy(h, q).wait_send()
            y_copy(h, q).wait_send()
            c_copy(h, q, 0).wait_send()
            c_copy(h, q, 1).wait_send()


def local_fast(sizes, attention, out_weight, task_tags, delta_values, block_rows, block_columns, block_live):
    n, owners = sizes["tensor"], sizes["task"]
    rows = attention.shape[0]
    depth, width = out_weight.shape
    owned, slots, hd = delta_values.shape[:3]
    blocks = width // hd
    chunk = width // n
    count = (n - 1) * (blocks // n)
    tags = jnp.broadcast_to(task_tags[:, None], (rows, 128))
    info = jnp.concatenate([block_rows, block_columns, block_live], axis=1).astype(jnp.bfloat16)
    table = jnp.broadcast_to(info[:, :, None], (owned, 3 * slots, 128)).reshape(owned, 3 * slots * 128)
    deltas = delta_values.transpose(1, 0, 2, 3).reshape(slots, PIECES, owned // PIECES * hd, hd)
    vmem = pl.BlockSpec(memory_space=pltpu.VMEM)
    hop = max(owners // 2 - 1, 1)
    dma = pltpu.SemaphoreType.DMA
    sends = [
        pltpu.VMEM((count, rows, 128), jnp.int16),
        pltpu.VMEM((count, 8, 128), jnp.float32),
    ]
    return pl.pallas_call(
        functools.partial(kernel, n, owners),
        out_shape=jax.ShapeDtypeStruct((rows, chunk), jnp.bfloat16),
        in_specs=[vmem, pl.BlockSpec(memory_space=pl.ANY), vmem, vmem, vmem],
        out_specs=vmem,
        scratch_shapes=[
            pltpu.VMEM((blocks, rows, 128), jnp.float32),
            pltpu.VMEM((RING, depth, WIDE), jnp.bfloat16),
            pltpu.VMEM((owners * owned, 3 * slots * 128), jnp.bfloat16),
            pltpu.VMEM((rows, 3 * slots * 128), jnp.float32),
            pltpu.VMEM((slots, rows, 128), jnp.float32),
            pltpu.VMEM((slots, rows, 128), jnp.float32),
            pltpu.VMEM((owners, slots, PIECES, owned // PIECES * hd, hd), jnp.bfloat16),
            pltpu.VMEM((rows, owned // PIECES * hd), jnp.bfloat16),
            *(sends * 4),
            dma((RING,)),
            dma((owners,)), dma((owners,)), dma, dma,
            dma((hop, PIECES)), dma((hop, PIECES)), dma((hop, PIECES)), dma((hop, PIECES)),
            dma((2, hop, PIECES)), dma((2, hop, PIECES)),
            *([dma((count,))] * 8),
        ],
        compiler_params=pltpu.CompilerParams(
            collective_id=0, has_side_effects=True, vmem_limit_bytes=60 * 1024 * 1024
        ),
        cost_estimate=pl.CostEstimate(
            flops=2 * rows * depth * width, bytes_accessed=2 * depth * width, transcendentals=0
        ),
    )(attention, out_weight, tags, table, deltas)


def solution(mesh):
    in_specs = (
        P(("groups", "task"), "tensor"),
        P("tensor", None),
        P(("groups", "task")),
        P("task", "tensor", None, None),
        P("task", "tensor"),
        P("task", "tensor"),
        P("task", "tensor"),
    )
    out_specs = P(("groups", "task"), "tensor")
    fast = fits(mesh)
    local = functools.partial(local_fast, mesh.shape) if fast else local_general
    return jax.shard_map(local, mesh=mesh, in_specs=in_specs, out_specs=out_specs, check_vma=False)
```

```python
import functools

import jax
import jax.numpy as jnp
from jax import lax
from jax.experimental import pallas as pl
from jax.experimental.pallas import tpu as pltpu
from jax.sharding import PartitionSpec as P


def pick(lookup, onehot):
    return jnp.sum(onehot * lookup, axis=-1)


def select_head(shard_heads, head_index):
    head_hits = (head_index[..., None] == jnp.arange(shard_heads.shape[-2])).astype(jnp.bfloat16)
    return jnp.einsum(
        "...hd,...h->...d", shard_heads, head_hits, preferred_element_type=jnp.float32
    ).astype(jnp.bfloat16)


def local_general(attention, out_weight, task_tags, delta_values, block_rows, block_columns, block_live):
    rows_count = attention.shape[0]
    width = out_weight.shape[1]
    head_dim = delta_values.shape[-1]
    per_shard = attention.shape[1] // head_dim
    owned_tasks = delta_values.shape[0]
    slot_count = delta_values.shape[1]
    col_blocks = width // head_dim
    owners = lax.axis_size("task")
    capacity = rows_count * 3 // 8
    owner_ids = task_tags // owned_tasks
    member = (owner_ids[:, None] == jnp.arange(owners)[None, :]).astype(jnp.int32)
    bucket_rank = jnp.sum(jnp.cumsum(member, axis=0) * member, axis=1) - 1
    placing = owner_ids * capacity + bucket_rank
    slot_tasks = (
        jnp.full((owners * capacity,), -1, jnp.int32)
        .at[placing]
        .set(task_tags - owner_ids * owned_tasks)
        .reshape(owners, capacity)
    )
    sending = (
        jnp.zeros((owners * capacity, attention.shape[1]), jnp.bfloat16).at[placing].set(attention)
    )
    sending = sending.reshape(owners, capacity, attention.shape[1])
    rows_in = lax.all_to_all(sending, "task", split_axis=0, concat_axis=0, tiled=True)
    task_ids = lax.all_to_all(slot_tasks, "task", split_axis=0, concat_axis=0, tiled=True)
    member_own = (task_ids[..., None] == jnp.arange(owned_tasks)).astype(jnp.int32)
    member_bf = member_own.astype(jnp.bfloat16)
    heads_in = rows_in.reshape(rows_in.shape[0], rows_in.shape[1], per_shard, head_dim)
    results = []
    found = []
    for slot_index in range(slot_count):
        chosen = select_head(heads_in, pick(block_rows[:, slot_index], member_own))
        spread = chosen[:, :, None, :] * member_bf[..., None]
        product = jnp.einsum(
            "abtd,tde->abe", spread, delta_values[:, slot_index], preferred_element_type=jnp.float32
        )
        results.append(
            product * pick(block_live[:, slot_index], member_own).astype(jnp.float32)[..., None]
        )
        found.append(pick(block_columns[:, slot_index], member_own))
    values_back = lax.all_to_all(
        jnp.stack(results, axis=2), "task", split_axis=0, concat_axis=0, tiled=True
    )
    columns_back = lax.all_to_all(
        jnp.stack(found, axis=2), "task", split_axis=0, concat_axis=0, tiled=True
    )
    values = values_back.reshape(owners * capacity, slot_count, head_dim)[placing]
    columns = columns_back.reshape(owners * capacity, slot_count)[placing]
    column_hits = (columns[:, :, None] == jnp.arange(col_blocks)).astype(jnp.float32)
    placed_delta = jnp.einsum(
        "rkc,rkd->cdr", column_hits, values, precision=lax.Precision.HIGHEST
    ).reshape(width, rows_count)
    base_part = lax.dot_general(
        out_weight, attention, (((0,), (1,)), ((), ())), preferred_element_type=jnp.float32
    )
    summed = lax.psum_scatter(base_part + placed_delta, "tensor", scatter_dimension=0, tiled=True)
    return summed.T.astype(jnp.bfloat16)


MESH = pl.DeviceIdType.MESH
PIECES = 4
RING = 4
WIDE = 256
LEVELS = 32766.0


def fits(mesh):
    shards = mesh.shape["tensor"]
    return 5120 % (shards * 256) == 0 and mesh.shape["groups"] == 2 and mesh.shape["task"] % 2 == 0


def kernel(
    n, owners, att_ref, w_ref, tag_ref, row_ref, col_ref, live_ref, delta_ref, out_ref,
    part, wbuf, tagf, tab, tab_all, ctab, ctab_in, onehot_info, chosen, vals, dbuf, spread,
    vsend, vscale, vrecv, vrscale, far_vals, far_cols,
    fsend, fscale, frecv, frscale, bsend, bscale, brecv, brscale,
    wsem, tab_ssem, tab_rsem, own_ssem, own_rsem,
    x_ssem, x_rsem, y_ssem, y_rsem, c_ssem, c_rsem,
    f_ssem, f_rsem, fs_ssem, fs_rsem, b_ssem, b_rsem, bs_ssem, bs_rsem,
    v_ssem, v_rsem, vs_ssem, vs_rsem, ct_ssem, ct_rsem,
):
    rows = att_ref.shape[0]
    blocks = part.shape[0]
    per = blocks // n
    g = lax.axis_index("groups")
    t = lax.axis_index("task")
    z = lax.axis_index("tensor")
    twin = t + 1 - 2 * lax.rem(t, 2)
    hops = range(2, owners, 2)
    owned = row_ref.shape[0]
    steps = blocks * 128 // WIDE
    chunk_steps = steps // n
    far = z // (n - 1)

    def step_at(i):
        return (i + chunk_steps * (n - 1) * (1 - far)) % steps

    def wcopy(i):
        slot = lax.rem(i, RING)
        at = step_at(i)
        return pltpu.make_async_copy(
            w_ref.at[:, pl.ds(pl.multiple_of(at * WIDE, WIDE), WIDE)], wbuf.at[slot], wsem.at[slot]
        )

    for i in range(RING - 1):
        wcopy(i).start()

    barrier = pltpu.get_barrier_semaphore()
    for k in range(1, owners):
        pl.semaphore_signal(barrier, 1, device_id={"task": lax.rem(t + k, owners)}, device_id_type=MESH)
    pl.semaphore_signal(barrier, 1, device_id={"groups": 1 - g}, device_id_type=MESH)

    for k in range(1, n):
        pl.semaphore_signal(barrier, 1, device_id={"tensor": lax.rem(z + k, n)}, device_id_type=MESH)
    pl.semaphore_wait(barrier, owners + n - 1)

    def remote(src, dst, ssem, rsem, where):
        return pltpu.make_async_remote_copy(
            src_ref=src, dst_ref=dst, send_sem=ssem, recv_sem=rsem, device_id=where, device_id_type=MESH
        )

    def tab_copy(k):
        here = tab_all.at[pl.ds(pl.multiple_of(t * owned, owned), owned)]
        return remote(tab, here, tab_ssem.at[k], tab_rsem.at[k], {"task": lax.rem(t + k, owners)})

    def x_copy(h, q):
        return remote(
            delta_ref.at[g, q], dbuf.at[t, g, q], x_ssem.at[h, q], x_rsem.at[h, q],
            {"task": lax.rem(t + 2 * h + 2, owners)},
        )

    def y_copy(h, q):
        src = lax.rem(t - 2 * h - 2 + owners, owners)
        return remote(
            dbuf.at[src, g, q], dbuf.at[src, g, q], y_ssem.at[h, q], y_rsem.at[h, q], {"groups": 1 - g}
        )

    def c_copy(h, q, half):
        src = lax.rem(t - 2 * h - 2 + owners, owners)
        slot = g if half == 0 else 1 - g
        return remote(
            dbuf.at[src, slot, q], dbuf.at[src, slot, q], c_ssem.at[half, h, q], c_rsem.at[half, h, q],
            {"task": twin},
        )

    for piece, ref in enumerate((row_ref, col_ref, live_ref)):
        for s in range(2):
            column = ref[:, s : s + 1].astype(jnp.float32)
            at = (2 * piece + s) * 128
            tab[:, at : at + 128] = jnp.broadcast_to(column, (owned, 128)).astype(jnp.bfloat16)

    own_copy = remote(delta_ref, dbuf.at[t], own_ssem, own_rsem, {"task": twin})
    for k in range(1, owners):
        tab_copy(k).start()
    for q in range(PIECES):
        for h in range(len(hops)):
            x_copy(h, q).start()
    own_copy.start()
    tab_all[pl.ds(pl.multiple_of(t * owned, owned), owned), :] = tab[...]

    def base_step(i, carry):
        @pl.when(i + RING - 1 < steps)
        def _():
            wcopy(i + RING - 1).start()

        wcopy(i).wait()
        got = jnp.dot(att_ref[...], wbuf[lax.rem(i, RING)], preferred_element_type=jnp.float32)
        for e in range(WIDE // 128):
            part[step_at(i) * (WIDE // 128) + e] = got[:, e * 128 : (e + 1) * 128]
        return carry

    def decoded(ref, scales, i):
        whole = ref[i].astype(jnp.int32).astype(jnp.float32).reshape(rows // 8, 8, 128)
        return (whole * scales[i][None]).reshape(rows, 128)

    def encode(total, ref, scales, i):
        cut = total.reshape(rows // 8, 8, 128)
        top = jnp.maximum(jnp.max(jnp.abs(cut), axis=0), 1e-30)
        scales[i] = top * (1.0 / LEVELS)
        levels = jnp.round(cut * (LEVELS / top)[None]).reshape(rows, 128)
        ref[i] = levels.astype(jnp.int32).astype(jnp.int16)

    def f_copies(i):
        where = {"tensor": z + 1}
        return (
            remote(fsend.at[i], frecv.at[i], f_ssem.at[i], f_rsem.at[i], where),
            remote(fscale.at[i], frscale.at[i], fs_ssem.at[i], fs_rsem.at[i], where),
        )

    def b_copies(i):
        where = {"tensor": z - 1}
        return (
            remote(bsend.at[i], brecv.at[i], b_ssem.at[i], b_rsem.at[i], where),
            remote(bscale.at[i], brscale.at[i], bs_ssem.at[i], bs_rsem.at[i], where),
        )

    def near_end(i, carry):
        @pl.when(z == 0)
        def _():
            encode(part[(n - 1) * per + i], fsend, fscale, i)
            for copy in f_copies(i):
                copy.start()

        @pl.when(z == n - 1)
        def _():
            encode(part[i], bsend, bscale, i)
            for copy in b_copies(i):
                copy.start()

        return carry

    for q in range(PIECES):
        lax.fori_loop(steps * q // PIECES, steps * (q + 1) // PIECES, base_step, 0)
        if (q + 1) * n >= PIECES and q * n < PIECES:
            lax.fori_loop(0, per, near_end, 0)
        for h in range(len(hops)):
            x_copy(h, q).wait_recv()
            y_copy(h, q).start()
            c_copy(h, q, 0).start()

    for k in range(1, owners):
        tab_copy(k).wait_recv()
    tasks = tab_all.shape[0]
    for i in range(rows // 128):
        line = jnp.broadcast_to(tag_ref[i : i + 1, :].astype(jnp.float32), (128, 128))
        tagf[i * 128 : (i + 1) * 128, :] = line.T
    hits = tagf[:, :tasks] == lax.broadcasted_iota(jnp.int32, (rows, tasks), 1).astype(jnp.float32)
    onehot = jnp.where(hits, 1.0, 0.0).astype(jnp.bfloat16)
    ctab[...] = tab_all[:, 256:512]
    onehot_info[...] = jnp.dot(onehot, tab_all[...], preferred_element_type=jnp.float32)
    tile = 64

    def choose(i, carry):
        at = pl.ds(pl.multiple_of(i * tile, tile), tile)
        heads = [onehot_info[at, s * 128 : (s + 1) * 128] for s in range(2)]
        picked = [jnp.zeros((tile, 128), jnp.float32) for s in range(2)]
        for h in range(att_ref.shape[1] // 128):
            block = att_ref[at, h * 128 : (h + 1) * 128].astype(jnp.float32)
            for s in range(2):
                picked[s] = jnp.where(heads[s] == float(h), block, picked[s])
        for s in range(2):
            chosen[s, at, :] = picked[s]
        return carry

    lax.fori_loop(0, rows // tile, choose, 0)
    vals[...] = jnp.zeros_like(vals)

    def add_half(ref, owner, half):
        each = owned // 2 // PIECES

        def body(q, carry):
            for s in range(2):
                for e in range(each):
                    task = owner * owned + half * (owned // 2) + q * each + e
                    spread[:, e * 128 : (e + 1) * 128] = jnp.where(
                        tagf[...] == task.astype(jnp.float32), chosen[s], 0.0
                    ).astype(jnp.bfloat16)
                source = ref[half, q, :, s].reshape(each * 128, 128)
                vals[s] += jnp.dot(spread[...], source, preferred_element_type=jnp.float32)
            return carry

        lax.fori_loop(0, PIECES, body, 0)

    for half in range(2):
        add_half(delta_ref, t, half)
    own_copy.wait_recv()
    for half in range(2):
        add_half(dbuf.at[twin], twin, half)
    for h in range(len(hops)):
        src = lax.rem(t - 2 * h - 2 + owners, owners)
        add_half(dbuf.at[src], src, g)
    for q in range(PIECES):
        for h in range(len(hops)):
            y_copy(h, q).wait_recv()
            c_copy(h, q, 1).start()
    for h in range(len(hops)):
        src = lax.rem(t - 2 * h - 2 + owners, owners)
        add_half(dbuf.at[src], src, 1 - g)
        other = lax.rem(twin - 2 * h - 2 + owners, owners)
        for q in range(PIECES):
            c_copy(h, q, 0).wait_recv()
            c_copy(h, q, 1).wait_recv()
        for half in range(2):
            add_half(dbuf.at[other], other, half)
    for s in range(2):
        vals[s] = vals[s] * onehot_info[:, (4 + s) * 128 : (5 + s) * 128]

    for s in range(2):
        encode(vals[s], vsend, vscale, s)

    def v_copies(end):
        where = {"tensor": end * (n - 1)}
        return (
            remote(vsend, vrecv.at[z], v_ssem.at[end], v_rsem.at[z], where),
            remote(vscale, vrscale.at[z], vs_ssem.at[end], vs_rsem.at[z], where),
            remote(ctab, ctab_in.at[z], ct_ssem.at[end], ct_rsem.at[z], where),
        )

    def v_arrivals(src):
        return (
            remote(vsend, vrecv.at[src], v_ssem.at[0], v_rsem.at[src], {"tensor": src}),
            remote(vscale, vrscale.at[src], vs_ssem.at[0], vs_rsem.at[src], {"tensor": src}),
            remote(ctab, ctab_in.at[src], ct_ssem.at[0], ct_rsem.at[src], {"tensor": src}),
        )

    @pl.when(z > 0)
    def _():
        for copy in v_copies(0):
            copy.start()

    @pl.when(z < n - 1)
    def _():
        for copy in v_copies(1):
            copy.start()

    def block_sum(c):
        total = part[c]
        for s in range(2):
            mine = onehot_info[:, (2 + s) * 128 : (3 + s) * 128] == c.astype(jnp.float32)
            total = total + jnp.where(mine, vals[s], 0.0)
        return total

    f_count = (n - 1 - z) * per
    b_count = z * per

    def chain(first, i, carry):
        @pl.when(i < f_count)
        def _():
            at = (n - 1 - i // per) * per + i % per
            base = (lambda: part[at]) if first else (lambda: block_sum(at))

            @pl.when(z > 0)
            def _():
                for copy in f_copies(i):
                    copy.wait_recv()
                encode(base() + decoded(frecv, frscale, i), fsend, fscale, i)
                for copy in f_copies(i):
                    copy.start()

            if not first:
                @pl.when(z == 0)
                def _():
                    encode(base(), fsend, fscale, i)
                    for copy in f_copies(i):
                        copy.start()

        @pl.when(i < b_count)
        def _():
            base = (lambda: part[i]) if first else (lambda: block_sum(i))

            @pl.when(z < n - 1)
            def _():
                for copy in b_copies(i):
                    copy.wait_recv()
                encode(base() + decoded(brecv, brscale, i), bsend, bscale, i)
                for copy in b_copies(i):
                    copy.start()

            if not first:
                @pl.when(z == n - 1)
                def _():
                    encode(base(), bsend, bscale, i)
                    for copy in b_copies(i):
                        copy.start()

        return carry

    lax.fori_loop(0, per, functools.partial(chain, True), 0)
    lax.fori_loop(per, (n - 1) * per, functools.partial(chain, False), 0)

    def far_source(end):
        for k in range(n - 1):
            src = k + 1 if end == 0 else k
            for copy in v_arrivals(src):
                copy.wait_recv()
            for s in range(2):
                whole = vrecv[src, s].astype(jnp.int32).astype(jnp.float32).reshape(rows // 8, 8, 128)
                far_vals[k, s] = (whole * vrscale[src, s][None]).reshape(rows, 128)
            far_cols[k] = jnp.dot(onehot_again(), ctab_in[src], preferred_element_type=jnp.float32)

    def onehot_again():
        found = tagf[:, :tasks] == lax.broadcasted_iota(jnp.int32, (rows, tasks), 1).astype(jnp.float32)
        return jnp.where(found, 1.0, 0.0).astype(jnp.bfloat16)

    @pl.when(z == 0)
    def _():
        far_source(0)

    @pl.when(z == n - 1)
    def _():
        far_source(1)

    def finish(j, carry):
        part[z * per + j] = block_sum(z * per + j)

        @pl.when((z == 0) | (z == n - 1))
        def _():
            at = (z * per + j).astype(jnp.float32)
            for k in range(n - 1):
                for s in range(2):
                    there = far_cols[k, :, s * 128 : (s + 1) * 128] == at
                    part[z * per + j] += jnp.where(there, far_vals[k, s], 0.0)

        @pl.when(z < n - 1)
        def _():
            i = z * per + j
            for copy in b_copies(i):
                copy.wait_recv()
            part[z * per + j] += decoded(brecv, brscale, i)

        @pl.when(z > 0)
        def _():
            i = (n - 1 - z) * per + j
            for copy in f_copies(i):
                copy.wait_recv()
            part[z * per + j] += decoded(frecv, frscale, i)

        out_ref[:, pl.ds(pl.multiple_of(j * 128, 128), 128)] = part[z * per + j].astype(out_ref.dtype)
        return carry

    lax.fori_loop(0, per, finish, 0)

    def drain(i, carry):
        @pl.when(i < f_count)
        def _():
            for copy in f_copies(i):
                copy.wait_send()

        @pl.when(i < b_count)
        def _():
            for copy in b_copies(i):
                copy.wait_send()

        return carry

    lax.fori_loop(0, (n - 1) * per, drain, 0)
    @pl.when(z > 0)
    def _():
        for copy in v_copies(0):
            copy.wait_send()

    @pl.when(z < n - 1)
    def _():
        for copy in v_copies(1):
            copy.wait_send()

    for k in range(1, owners):
        tab_copy(k).wait_send()
    own_copy.wait_send()
    for q in range(PIECES):
        for h in range(len(hops)):
            x_copy(h, q).wait_send()
            y_copy(h, q).wait_send()
            c_copy(h, q, 0).wait_send()
            c_copy(h, q, 1).wait_send()


def local_fast(sizes, attention, out_weight, task_tags, delta_values, block_rows, block_columns, block_live):
    n, owners = sizes["tensor"], sizes["task"]
    rows = attention.shape[0]
    depth, width = out_weight.shape
    owned, slots, hd = delta_values.shape[:3]
    blocks = width // hd
    chunk = width // n
    count = (n - 1) * (blocks // n)
    tags = task_tags.reshape(rows // 128, 128)
    deltas = delta_values.reshape(2, PIECES, owned // (2 * PIECES), slots, hd, hd)
    vmem = pl.BlockSpec(memory_space=pltpu.VMEM)
    hop = max(owners // 2 - 1, 1)
    dma = pltpu.SemaphoreType.DMA
    sends = [
        pltpu.VMEM((count, rows, 128), jnp.int16),
        pltpu.VMEM((count, 8, 128), jnp.float32),
    ]
    return pl.pallas_call(
        functools.partial(kernel, n, owners),
        out_shape=jax.ShapeDtypeStruct((rows, chunk), jnp.bfloat16),
        in_specs=[vmem, pl.BlockSpec(memory_space=pl.ANY), vmem, vmem, vmem, vmem, vmem],
        out_specs=vmem,
        scratch_shapes=[
            pltpu.VMEM((blocks, rows, 128), jnp.float32),
            pltpu.VMEM((RING, depth, WIDE), jnp.bfloat16),
            pltpu.VMEM((rows, 128), jnp.float32),
            pltpu.VMEM((owned, 3 * slots * 128), jnp.bfloat16),
            pltpu.VMEM((owners * owned, 3 * slots * 128), jnp.bfloat16),
            pltpu.VMEM((owners * owned, slots * 128), jnp.bfloat16),
            pltpu.VMEM((n, owners * owned, slots * 128), jnp.bfloat16),
            pltpu.VMEM((rows, 3 * slots * 128), jnp.float32),
            pltpu.VMEM((slots, rows, 128), jnp.float32),
            pltpu.VMEM((slots, rows, 128), jnp.float32),
            pltpu.VMEM((owners, *deltas.shape), jnp.bfloat16),
            pltpu.VMEM((rows, owned // (2 * PIECES) * hd), jnp.bfloat16),
            pltpu.VMEM((slots, rows, 128), jnp.int16),
            pltpu.VMEM((slots, 8, 128), jnp.float32),
            pltpu.VMEM((n, slots, rows, 128), jnp.int16),
            pltpu.VMEM((n, slots, 8, 128), jnp.float32),
            pltpu.VMEM((n - 1, slots, rows, 128), jnp.float32),
            pltpu.VMEM((n - 1, rows, slots * 128), jnp.float32),
            *(sends * 4),
            dma((RING,)),
            dma((owners,)), dma((owners,)), dma, dma,
            dma((hop, PIECES)), dma((hop, PIECES)), dma((hop, PIECES)), dma((hop, PIECES)),
            dma((2, hop, PIECES)), dma((2, hop, PIECES)),
            *([dma((count,))] * 8),
            *([dma((2,)), dma((n,))] * 3),
        ],
        compiler_params=pltpu.CompilerParams(
            collective_id=0, has_side_effects=True, vmem_limit_bytes=60 * 1024 * 1024
        ),
        cost_estimate=pl.CostEstimate(
            flops=2 * rows * depth * width, bytes_accessed=2 * depth * width, transcendentals=0
        ),
    )(attention, out_weight, tags, block_rows, block_columns, block_live, deltas)


def solution(mesh):
    in_specs = (
        P(("groups", "task"), "tensor"),
        P("tensor", None),
        P(("groups", "task")),
        P("task", "tensor", None, None),
        P("task", "tensor"),
        P("task", "tensor"),
        P("task", "tensor"),
    )
    out_specs = P(("groups", "task"), "tensor")
    fast = fits(mesh)
    local = functools.partial(local_fast, mesh.shape) if fast else local_general
    return jax.shard_map(local, mesh=mesh, in_specs=in_specs, out_specs=out_specs, check_vma=False)
```

```python
import functools

import jax
import jax.numpy as jnp
from jax import lax
from jax.experimental import pallas as pl
from jax.experimental.pallas import tpu as pltpu
from jax.sharding import PartitionSpec as P


def pick(lookup, onehot):
    return jnp.sum(onehot * lookup, axis=-1)


def select_head(shard_heads, head_index):
    head_hits = (head_index[..., None] == jnp.arange(shard_heads.shape[-2])).astype(jnp.bfloat16)
    return jnp.einsum(
        "...hd,...h->...d", shard_heads, head_hits, preferred_element_type=jnp.float32
    ).astype(jnp.bfloat16)


def local_general(attention, out_weight, task_tags, delta_values, block_rows, block_columns, block_live):
    rows_count = attention.shape[0]
    width = out_weight.shape[1]
    head_dim = delta_values.shape[-1]
    per_shard = attention.shape[1] // head_dim
    owned_tasks = delta_values.shape[0]
    slot_count = delta_values.shape[1]
    col_blocks = width // head_dim
    owners = lax.axis_size("task")
    capacity = rows_count * 3 // 8
    owner_ids = task_tags // owned_tasks
    member = (owner_ids[:, None] == jnp.arange(owners)[None, :]).astype(jnp.int32)
    bucket_rank = jnp.sum(jnp.cumsum(member, axis=0) * member, axis=1) - 1
    placing = owner_ids * capacity + bucket_rank
    slot_tasks = (
        jnp.full((owners * capacity,), -1, jnp.int32)
        .at[placing]
        .set(task_tags - owner_ids * owned_tasks)
        .reshape(owners, capacity)
    )
    sending = (
        jnp.zeros((owners * capacity, attention.shape[1]), jnp.bfloat16).at[placing].set(attention)
    )
    sending = sending.reshape(owners, capacity, attention.shape[1])
    rows_in = lax.all_to_all(sending, "task", split_axis=0, concat_axis=0, tiled=True)
    task_ids = lax.all_to_all(slot_tasks, "task", split_axis=0, concat_axis=0, tiled=True)
    member_own = (task_ids[..., None] == jnp.arange(owned_tasks)).astype(jnp.int32)
    member_bf = member_own.astype(jnp.bfloat16)
    heads_in = rows_in.reshape(rows_in.shape[0], rows_in.shape[1], per_shard, head_dim)
    results = []
    found = []
    for slot_index in range(slot_count):
        chosen = select_head(heads_in, pick(block_rows[:, slot_index], member_own))
        spread = chosen[:, :, None, :] * member_bf[..., None]
        product = jnp.einsum(
            "abtd,tde->abe", spread, delta_values[:, slot_index], preferred_element_type=jnp.float32
        )
        results.append(
            product * pick(block_live[:, slot_index], member_own).astype(jnp.float32)[..., None]
        )
        found.append(pick(block_columns[:, slot_index], member_own))
    values_back = lax.all_to_all(
        jnp.stack(results, axis=2), "task", split_axis=0, concat_axis=0, tiled=True
    )
    columns_back = lax.all_to_all(
        jnp.stack(found, axis=2), "task", split_axis=0, concat_axis=0, tiled=True
    )
    values = values_back.reshape(owners * capacity, slot_count, head_dim)[placing]
    columns = columns_back.reshape(owners * capacity, slot_count)[placing]
    column_hits = (columns[:, :, None] == jnp.arange(col_blocks)).astype(jnp.float32)
    placed_delta = jnp.einsum(
        "rkc,rkd->cdr", column_hits, values, precision=lax.Precision.HIGHEST
    ).reshape(width, rows_count)
    base_part = lax.dot_general(
        out_weight, attention, (((0,), (1,)), ((), ())), preferred_element_type=jnp.float32
    )
    summed = lax.psum_scatter(base_part + placed_delta, "tensor", scatter_dimension=0, tiled=True)
    return summed.T.astype(jnp.bfloat16)


MESH = pl.DeviceIdType.MESH
PIECES = 4
RING = 4
WIDE = 256
LEVELS = 32766.0
PAIR = WIDE // 128


def fits(mesh):
    shards = mesh.shape["tensor"]
    return shards > 1 and 5120 % (shards * 256) == 0 and mesh.shape["groups"] == 2 and mesh.shape["task"] % 2 == 0


def kernel(
    n, owners, att_ref, w_ref, tag_ref, row_ref, col_ref, live_ref, delta_ref, out_ref,
    part, wbuf, tagf, tab, tab_all, ctab, ctab_in, onehot_info, chosen, vals, dbuf, spread,
    vsend, vscale, vrecv, vrscale, far_vals, far_cols,
    fsend, fscale, frecv, frscale, bsend, bscale, brecv, brscale,
    wsem, tab_ssem, tab_rsem, own_ssem, own_rsem,
    x_ssem, x_rsem, y_ssem, y_rsem, c_ssem, c_rsem,
    f_ssem, f_rsem, fs_ssem, fs_rsem, b_ssem, b_rsem, bs_ssem, bs_rsem,
    v_ssem, v_rsem, vs_ssem, vs_rsem, ct_ssem, ct_rsem,
):
    rows = att_ref.shape[0]
    steps = part.shape[0]
    per = steps // n
    g = lax.axis_index("groups")
    t = lax.axis_index("task")
    z = lax.axis_index("tensor")
    twin = t + 1 - 2 * lax.rem(t, 2)
    hops = range(2, owners, 2)
    owned = row_ref.shape[0]
    far = z // (n - 1)

    def step_at(i):
        return (i + per * (n - 1) * (1 - far)) % steps

    def wcopy(i):
        slot = lax.rem(i, RING)
        at = step_at(i)
        return pltpu.make_async_copy(
            w_ref.at[:, pl.ds(pl.multiple_of(at * WIDE, WIDE), WIDE)], wbuf.at[slot], wsem.at[slot]
        )

    for i in range(RING - 1):
        wcopy(i).start()

    barrier = pltpu.get_barrier_semaphore()
    for k in range(1, owners):
        pl.semaphore_signal(barrier, 1, device_id={"task": lax.rem(t + k, owners)}, device_id_type=MESH)
    pl.semaphore_signal(barrier, 1, device_id={"groups": 1 - g}, device_id_type=MESH)

    for k in range(1, n):
        pl.semaphore_signal(barrier, 1, device_id={"tensor": lax.rem(z + k, n)}, device_id_type=MESH)
    pl.semaphore_wait(barrier, owners + n - 1)

    def remote(src, dst, ssem, rsem, where):
        return pltpu.make_async_remote_copy(
            src_ref=src, dst_ref=dst, send_sem=ssem, recv_sem=rsem, device_id=where, device_id_type=MESH
        )

    def tab_copy(k):
        here = tab_all.at[pl.ds(pl.multiple_of(t * owned, owned), owned)]
        return remote(tab, here, tab_ssem.at[k], tab_rsem.at[k], {"task": lax.rem(t + k, owners)})

    def x_copy(h, q):
        return remote(
            delta_ref.at[g, q], dbuf.at[t, g, q], x_ssem.at[h, q], x_rsem.at[h, q],
            {"task": lax.rem(t + 2 * h + 2, owners)},
        )

    def y_copy(h, q):
        src = lax.rem(t - 2 * h - 2 + owners, owners)
        return remote(
            dbuf.at[src, g, q], dbuf.at[src, g, q], y_ssem.at[h, q], y_rsem.at[h, q], {"groups": 1 - g}
        )

    def c_copy(h, q, half):
        src = lax.rem(t - 2 * h - 2 + owners, owners)
        slot = g if half == 0 else 1 - g
        return remote(
            dbuf.at[src, slot, q], dbuf.at[src, slot, q], c_ssem.at[half, h, q], c_rsem.at[half, h, q],
            {"task": twin},
        )

    for piece, ref in enumerate((row_ref, col_ref, live_ref)):
        for s in range(2):
            column = ref[:, s : s + 1].astype(jnp.float32)
            at = (2 * piece + s) * 128
            tab[:, at : at + 128] = jnp.broadcast_to(column, (owned, 128)).astype(jnp.bfloat16)

    own_copy = remote(delta_ref, dbuf.at[t], own_ssem, own_rsem, {"task": twin})
    for k in range(1, owners):
        tab_copy(k).start()
    for q in range(PIECES):
        for h in range(len(hops)):
            x_copy(h, q).start()
    own_copy.start()
    tab_all[pl.ds(pl.multiple_of(t * owned, owned), owned), :] = tab[...]

    def base_step(i, carry):
        @pl.when(i + RING - 1 < steps)
        def _():
            wcopy(i + RING - 1).start()

        wcopy(i).wait()
        got = jnp.dot(att_ref[...], wbuf[lax.rem(i, RING)], preferred_element_type=jnp.float32)
        for e in range(PAIR):
            part[step_at(i), e] = got[:, e * 128 : (e + 1) * 128]
        return carry

    def decoded(blocks, scale):
        whole = blocks.astype(jnp.int32).astype(jnp.float32).reshape(rows // 8, 8, 128)
        return (whole * scale[None]).reshape(rows, 128)

    def encode(total, ref, scales, at):
        cut = total.reshape(rows // 8, 8, 128)
        top = jnp.maximum(jnp.max(jnp.abs(cut), axis=0), 1e-30)
        scales[at] = top * (1.0 / LEVELS)
        levels = jnp.round(cut * (LEVELS / top)[None]).reshape(rows, 128)
        ref[at] = levels.astype(jnp.int32).astype(jnp.int16)

    def f_copies(i):
        where = {"tensor": z + 1}
        return (
            remote(fsend.at[i], frecv.at[i], f_ssem.at[i], f_rsem.at[i], where),
            remote(fscale.at[i], frscale.at[i], fs_ssem.at[i], fs_rsem.at[i], where),
        )

    def b_copies(i):
        where = {"tensor": z - 1}
        return (
            remote(bsend.at[i], brecv.at[i], b_ssem.at[i], b_rsem.at[i], where),
            remote(bscale.at[i], brscale.at[i], bs_ssem.at[i], bs_rsem.at[i], where),
        )

    def near_end(i, carry):
        @pl.when(z == 0)
        def _():
            for e in range(PAIR):
                encode(part[(n - 1) * per + i, e], fsend, fscale, (i, e))
            for copy in f_copies(i):
                copy.start()

        @pl.when(z == n - 1)
        def _():
            for e in range(PAIR):
                encode(part[i, e], bsend, bscale, (i, e))
            for copy in b_copies(i):
                copy.start()

        return carry

    for q in range(PIECES):
        lax.fori_loop(steps * q // PIECES, steps * (q + 1) // PIECES, base_step, 0)
        if (q + 1) * n >= PIECES and q * n < PIECES:
            lax.fori_loop(0, per, near_end, 0)
        for h in range(len(hops)):
            x_copy(h, q).wait_recv()
            y_copy(h, q).start()
            c_copy(h, q, 0).start()

    for k in range(1, owners):
        tab_copy(k).wait_recv()
    tasks = tab_all.shape[0]
    for i in range(rows // 128):
        line = jnp.broadcast_to(tag_ref[i : i + 1, :].astype(jnp.float32), (128, 128))
        tagf[i * 128 : (i + 1) * 128, :] = line.T
    hits = tagf[:, :tasks] == lax.broadcasted_iota(jnp.int32, (rows, tasks), 1).astype(jnp.float32)
    onehot = jnp.where(hits, 1.0, 0.0).astype(jnp.bfloat16)
    ctab[...] = tab_all[:, 256:512]
    onehot_info[...] = jnp.dot(onehot, tab_all[...], preferred_element_type=jnp.float32)
    tile = 64

    def choose(i, carry):
        at = pl.ds(pl.multiple_of(i * tile, tile), tile)
        heads = [onehot_info[at, s * 128 : (s + 1) * 128] for s in range(2)]
        picked = [jnp.zeros((tile, 128), jnp.float32) for s in range(2)]
        for h in range(att_ref.shape[1] // 128):
            block = att_ref[at, h * 128 : (h + 1) * 128].astype(jnp.float32)
            for s in range(2):
                picked[s] = jnp.where(heads[s] == float(h), block, picked[s])
        for s in range(2):
            chosen[s, at, :] = picked[s]
        return carry

    lax.fori_loop(0, rows // tile, choose, 0)
    vals[...] = jnp.zeros_like(vals)

    def add_half(ref, owner, half):
        each = owned // 2 // PIECES

        def body(q, carry):
            for s in range(2):
                for e in range(each):
                    task = owner * owned + half * (owned // 2) + q * each + e
                    spread[:, e * 128 : (e + 1) * 128] = jnp.where(
                        tagf[...] == task.astype(jnp.float32), chosen[s], 0.0
                    ).astype(jnp.bfloat16)
                source = ref[half, q, :, s].reshape(each * 128, 128)
                vals[s] += jnp.dot(spread[...], source, preferred_element_type=jnp.float32)
            return carry

        lax.fori_loop(0, PIECES, body, 0)

    for half in range(2):
        add_half(delta_ref, t, half)
    own_copy.wait_recv()
    for half in range(2):
        add_half(dbuf.at[twin], twin, half)
    for h in range(len(hops)):
        src = lax.rem(t - 2 * h - 2 + owners, owners)
        add_half(dbuf.at[src], src, g)
    for q in range(PIECES):
        for h in range(len(hops)):
            y_copy(h, q).wait_recv()
            c_copy(h, q, 1).start()
    for h in range(len(hops)):
        src = lax.rem(t - 2 * h - 2 + owners, owners)
        add_half(dbuf.at[src], src, 1 - g)
        other = lax.rem(twin - 2 * h - 2 + owners, owners)
        for q in range(PIECES):
            c_copy(h, q, 0).wait_recv()
            c_copy(h, q, 1).wait_recv()
        for half in range(2):
            add_half(dbuf.at[other], other, half)
    for s in range(2):
        vals[s] = vals[s] * onehot_info[:, (4 + s) * 128 : (5 + s) * 128]

    for s in range(2):
        encode(vals[s], vsend, vscale, s)

    def v_copies(end):
        where = {"tensor": end * (n - 1)}
        return (
            remote(vsend, vrecv.at[z], v_ssem.at[end], v_rsem.at[z], where),
            remote(vscale, vrscale.at[z], vs_ssem.at[end], vs_rsem.at[z], where),
            remote(ctab, ctab_in.at[z], ct_ssem.at[end], ct_rsem.at[z], where),
        )

    def v_arrivals(src):
        return (
            remote(vsend, vrecv.at[src], v_ssem.at[0], v_rsem.at[src], {"tensor": src}),
            remote(vscale, vrscale.at[src], vs_ssem.at[0], vs_rsem.at[src], {"tensor": src}),
            remote(ctab, ctab_in.at[src], ct_ssem.at[0], ct_rsem.at[src], {"tensor": src}),
        )

    @pl.when(z > 0)
    def _():
        for copy in v_copies(0):
            copy.start()

    @pl.when(z < n - 1)
    def _():
        for copy in v_copies(1):
            copy.start()

    def block_sum(c, e):
        total = part[c, e]
        block = (c * PAIR + e).astype(jnp.float32)
        for s in range(2):
            mine = onehot_info[:, (2 + s) * 128 : (3 + s) * 128] == block
            total = total + jnp.where(mine, vals[s], 0.0)
        return total

    f_count = (n - 1 - z) * per
    b_count = z * per

    def chain(first, i, carry):
        @pl.when(i < f_count)
        def _():
            at = (n - 1 - i // per) * per + i % per
            base = (lambda e: part[at, e]) if first else (lambda e: block_sum(at, e))

            @pl.when(z > 0)
            def _():
                for copy in f_copies(i):
                    copy.wait_recv()
                for e in range(PAIR):
                    encode(base(e) + decoded(frecv[i, e], frscale[i, e]), fsend, fscale, (i, e))
                for copy in f_copies(i):
                    copy.start()

            if not first:
                @pl.when(z == 0)
                def _():
                    for e in range(PAIR):
                        encode(base(e), fsend, fscale, (i, e))
                    for copy in f_copies(i):
                        copy.start()

        @pl.when(i < b_count)
        def _():
            base = (lambda e: part[i, e]) if first else (lambda e: block_sum(i, e))

            @pl.when(z < n - 1)
            def _():
                for copy in b_copies(i):
                    copy.wait_recv()
                for e in range(PAIR):
                    encode(base(e) + decoded(brecv[i, e], brscale[i, e]), bsend, bscale, (i, e))
                for copy in b_copies(i):
                    copy.start()

            if not first:
                @pl.when(z == n - 1)
                def _():
                    for e in range(PAIR):
                        encode(base(e), bsend, bscale, (i, e))
                    for copy in b_copies(i):
                        copy.start()

        return carry

    lax.fori_loop(0, per, functools.partial(chain, True), 0)
    lax.fori_loop(per, (n - 1) * per, functools.partial(chain, False), 0)

    def far_source(end):
        for k in range(n - 1):
            src = k + 1 if end == 0 else k
            for copy in v_arrivals(src):
                copy.wait_recv()
            for s in range(2):
                far_vals[k, s] = decoded(vrecv[src, s], vrscale[src, s])
            far_cols[k] = jnp.dot(onehot_again(), ctab_in[src], preferred_element_type=jnp.float32)

    def onehot_again():
        found = tagf[:, :tasks] == lax.broadcasted_iota(jnp.int32, (rows, tasks), 1).astype(jnp.float32)
        return jnp.where(found, 1.0, 0.0).astype(jnp.bfloat16)

    @pl.when(z == 0)
    def _():
        far_source(0)

    @pl.when(z == n - 1)
    def _():
        far_source(1)

    def finish(j, carry):
        c = z * per + j
        for e in range(PAIR):
            part[c, e] = block_sum(c, e)

        @pl.when((z == 0) | (z == n - 1))
        def _():
            for e in range(PAIR):
                block = (c * PAIR + e).astype(jnp.float32)
                for k in range(n - 1):
                    for s in range(2):
                        there = far_cols[k, :, s * 128 : (s + 1) * 128] == block
                        part[c, e] += jnp.where(there, far_vals[k, s], 0.0)

        @pl.when(z < n - 1)
        def _():
            i = z * per + j
            for copy in b_copies(i):
                copy.wait_recv()
            for e in range(PAIR):
                part[c, e] += decoded(brecv[i, e], brscale[i, e])

        @pl.when(z > 0)
        def _():
            i = (n - 1 - z) * per + j
            for copy in f_copies(i):
                copy.wait_recv()
            for e in range(PAIR):
                part[c, e] += decoded(frecv[i, e], frscale[i, e])

        for e in range(PAIR):
            at = pl.ds(pl.multiple_of(j * WIDE + e * 128, 128), 128)
            out_ref[:, at] = part[c, e].astype(out_ref.dtype)
        return carry

    lax.fori_loop(0, per, finish, 0)

    def drain(i, carry):
        @pl.when(i < f_count)
        def _():
            for copy in f_copies(i):
                copy.wait_send()

        @pl.when(i < b_count)
        def _():
            for copy in b_copies(i):
                copy.wait_send()

        return carry

    lax.fori_loop(0, (n - 1) * per, drain, 0)
    @pl.when(z > 0)
    def _():
        for copy in v_copies(0):
            copy.wait_send()

    @pl.when(z < n - 1)
    def _():
        for copy in v_copies(1):
            copy.wait_send()

    for k in range(1, owners):
        tab_copy(k).wait_send()
    own_copy.wait_send()
    for q in range(PIECES):
        for h in range(len(hops)):
            x_copy(h, q).wait_send()
            y_copy(h, q).wait_send()
            c_copy(h, q, 0).wait_send()
            c_copy(h, q, 1).wait_send()


def local_fast(sizes, attention, out_weight, task_tags, delta_values, block_rows, block_columns, block_live):
    n, owners = sizes["tensor"], sizes["task"]
    rows = attention.shape[0]
    depth, width = out_weight.shape
    owned, slots, hd = delta_values.shape[:3]
    steps = width // WIDE
    chunk = width // n
    count = (n - 1) * (steps // n)
    tags = task_tags.reshape(rows // 128, 128)
    deltas = delta_values.reshape(2, PIECES, owned // (2 * PIECES), slots, hd, hd)
    vmem = pl.BlockSpec(memory_space=pltpu.VMEM)
    hop = max(owners // 2 - 1, 1)
    dma = pltpu.SemaphoreType.DMA
    sends = [
        pltpu.VMEM((count, PAIR, rows, 128), jnp.int16),
        pltpu.VMEM((count, PAIR, 8, 128), jnp.float32),
    ]
    return pl.pallas_call(
        functools.partial(kernel, n, owners),
        out_shape=jax.ShapeDtypeStruct((rows, chunk), jnp.bfloat16),
        in_specs=[vmem, pl.BlockSpec(memory_space=pl.ANY), vmem, vmem, vmem, vmem, vmem],
        out_specs=vmem,
        scratch_shapes=[
            pltpu.VMEM((steps, PAIR, rows, 128), jnp.float32),
            pltpu.VMEM((RING, depth, WIDE), jnp.bfloat16),
            pltpu.VMEM((rows, 128), jnp.float32),
            pltpu.VMEM((owned, 3 * slots * 128), jnp.bfloat16),
            pltpu.VMEM((owners * owned, 3 * slots * 128), jnp.bfloat16),
            pltpu.VMEM((owners * owned, slots * 128), jnp.bfloat16),
            pltpu.VMEM((n, owners * owned, slots * 128), jnp.bfloat16),
            pltpu.VMEM((rows, 3 * slots * 128), jnp.float32),
            pltpu.VMEM((slots, rows, 128), jnp.float32),
            pltpu.VMEM((slots, rows, 128), jnp.float32),
            pltpu.VMEM((owners, *deltas.shape), jnp.bfloat16),
            pltpu.VMEM((rows, owned // (2 * PIECES) * hd), jnp.bfloat16),
            pltpu.VMEM((slots, rows, 128), jnp.int16),
            pltpu.VMEM((slots, 8, 128), jnp.float32),
            pltpu.VMEM((n, slots, rows, 128), jnp.int16),
            pltpu.VMEM((n, slots, 8, 128), jnp.float32),
            pltpu.VMEM((n - 1, slots, rows, 128), jnp.float32),
            pltpu.VMEM((n - 1, rows, slots * 128), jnp.float32),
            *(sends * 4),
            dma((RING,)),
            dma((owners,)), dma((owners,)), dma, dma,
            dma((hop, PIECES)), dma((hop, PIECES)), dma((hop, PIECES)), dma((hop, PIECES)),
            dma((2, hop, PIECES)), dma((2, hop, PIECES)),
            *([dma((count,))] * 8),
            *([dma((2,)), dma((n,))] * 3),
        ],
        compiler_params=pltpu.CompilerParams(
            collective_id=0, has_side_effects=True, vmem_limit_bytes=60 * 1024 * 1024
        ),
        cost_estimate=pl.CostEstimate(
            flops=2 * rows * depth * width, bytes_accessed=2 * depth * width, transcendentals=0
        ),
    )(attention, out_weight, tags, block_rows, block_columns, block_live, deltas)


def solution(mesh):
    in_specs = (
        P(("groups", "task"), "tensor"),
        P("tensor", None),
        P(("groups", "task")),
        P("task", "tensor", None, None),
        P("task", "tensor"),
        P("task", "tensor"),
        P("task", "tensor"),
    )
    out_specs = P(("groups", "task"), "tensor")
    fast = fits(mesh)
    local = functools.partial(local_fast, mesh.shape) if fast else local_general
    return jax.shard_map(local, mesh=mesh, in_specs=in_specs, out_specs=out_specs, check_vma=False)
```

```python
import functools

import jax
import jax.numpy as jnp
from jax import lax
from jax.experimental import pallas as pl
from jax.experimental.pallas import tpu as pltpu
from jax.sharding import PartitionSpec as P


def pick(lookup, onehot):
    return jnp.sum(onehot * lookup, axis=-1)


def select_head(shard_heads, head_index):
    head_hits = (head_index[..., None] == jnp.arange(shard_heads.shape[-2])).astype(jnp.bfloat16)
    return jnp.einsum(
        "...hd,...h->...d", shard_heads, head_hits, preferred_element_type=jnp.float32
    ).astype(jnp.bfloat16)


def local_general(attention, out_weight, task_tags, delta_values, block_rows, block_columns, block_live):
    rows_count = attention.shape[0]
    width = out_weight.shape[1]
    head_dim = delta_values.shape[-1]
    per_shard = attention.shape[1] // head_dim
    owned_tasks = delta_values.shape[0]
    slot_count = delta_values.shape[1]
    col_blocks = width // head_dim
    owners = lax.axis_size("task")
    capacity = rows_count * 3 // 8
    owner_ids = task_tags // owned_tasks
    member = (owner_ids[:, None] == jnp.arange(owners)[None, :]).astype(jnp.int32)
    bucket_rank = jnp.sum(jnp.cumsum(member, axis=0) * member, axis=1) - 1
    placing = owner_ids * capacity + bucket_rank
    slot_tasks = (
        jnp.full((owners * capacity,), -1, jnp.int32)
        .at[placing]
        .set(task_tags - owner_ids * owned_tasks)
        .reshape(owners, capacity)
    )
    sending = (
        jnp.zeros((owners * capacity, attention.shape[1]), jnp.bfloat16).at[placing].set(attention)
    )
    sending = sending.reshape(owners, capacity, attention.shape[1])
    rows_in = lax.all_to_all(sending, "task", split_axis=0, concat_axis=0, tiled=True)
    task_ids = lax.all_to_all(slot_tasks, "task", split_axis=0, concat_axis=0, tiled=True)
    member_own = (task_ids[..., None] == jnp.arange(owned_tasks)).astype(jnp.int32)
    member_bf = member_own.astype(jnp.bfloat16)
    heads_in = rows_in.reshape(rows_in.shape[0], rows_in.shape[1], per_shard, head_dim)
    results = []
    found = []
    for slot_index in range(slot_count):
        chosen = select_head(heads_in, pick(block_rows[:, slot_index], member_own))
        spread = chosen[:, :, None, :] * member_bf[..., None]
        product = jnp.einsum(
            "abtd,tde->abe", spread, delta_values[:, slot_index], preferred_element_type=jnp.float32
        )
        results.append(
            product * pick(block_live[:, slot_index], member_own).astype(jnp.float32)[..., None]
        )
        found.append(pick(block_columns[:, slot_index], member_own))
    values_back = lax.all_to_all(
        jnp.stack(results, axis=2), "task", split_axis=0, concat_axis=0, tiled=True
    )
    columns_back = lax.all_to_all(
        jnp.stack(found, axis=2), "task", split_axis=0, concat_axis=0, tiled=True
    )
    values = values_back.reshape(owners * capacity, slot_count, head_dim)[placing]
    columns = columns_back.reshape(owners * capacity, slot_count)[placing]
    column_hits = (columns[:, :, None] == jnp.arange(col_blocks)).astype(jnp.float32)
    placed_delta = jnp.einsum(
        "rkc,rkd->cdr", column_hits, values, precision=lax.Precision.HIGHEST
    ).reshape(width, rows_count)
    base_part = lax.dot_general(
        out_weight, attention, (((0,), (1,)), ((), ())), preferred_element_type=jnp.float32
    )
    summed = lax.psum_scatter(base_part + placed_delta, "tensor", scatter_dimension=0, tiled=True)
    return summed.T.astype(jnp.bfloat16)


MESH = pl.DeviceIdType.MESH
PIECES = 4
RING = 4
WIDE = 256
LEVELS = 32766.0
PAIR = WIDE // 128


def fits(mesh):
    shards = mesh.shape["tensor"]
    return shards > 1 and 5120 % (shards * 256) == 0 and mesh.shape["groups"] == 2 and mesh.shape["task"] % 2 == 0


def kernel(
    n, owners, att_ref, w_ref, tag_ref, row_ref, col_ref, live_ref, delta_ref, out_ref,
    part, wbuf, tagf, tab, tab_all, ctab, ctab_in, onehot_info, chosen, vals, dbuf, spread,
    vsend, vscale, vrecv, vrscale, far_vals, far_cols,
    fsend, fscale, frecv, frscale, bsend, bscale, brecv, brscale,
    wsem, tab_ssem, tab_rsem, own_ssem, own_rsem,
    x_ssem, x_rsem, y_ssem, y_rsem, c_ssem, c_rsem,
    f_ssem, f_rsem, fs_ssem, fs_rsem, b_ssem, b_rsem, bs_ssem, bs_rsem,
    v_ssem, v_rsem, vs_ssem, vs_rsem, ct_ssem, ct_rsem,
):
    rows = att_ref.shape[0]
    steps = part.shape[0]
    per = steps // n
    g = lax.axis_index("groups")
    t = lax.axis_index("task")
    z = lax.axis_index("tensor")
    twin = t + 1 - 2 * lax.rem(t, 2)
    hops = range(2, owners, 2)
    owned = row_ref.shape[0]
    far = z // (n - 1)

    def step_at(i):
        return (i + per * (n - 1) * (1 - far)) % steps

    def wcopy(i):
        slot = lax.rem(i, RING)
        at = step_at(i)
        return pltpu.make_async_copy(
            w_ref.at[:, pl.ds(pl.multiple_of(at * WIDE, WIDE), WIDE)], wbuf.at[slot], wsem.at[slot]
        )

    for i in range(RING - 1):
        wcopy(i).start()

    barrier = pltpu.get_barrier_semaphore()
    for k in range(1, owners):
        pl.semaphore_signal(barrier, 1, device_id={"task": lax.rem(t + k, owners)}, device_id_type=MESH)
    pl.semaphore_signal(barrier, 1, device_id={"groups": 1 - g}, device_id_type=MESH)

    for k in range(1, n):
        pl.semaphore_signal(barrier, 1, device_id={"tensor": lax.rem(z + k, n)}, device_id_type=MESH)
    pl.semaphore_wait(barrier, owners + n - 1)

    def remote(src, dst, ssem, rsem, where):
        return pltpu.make_async_remote_copy(
            src_ref=src, dst_ref=dst, send_sem=ssem, recv_sem=rsem, device_id=where, device_id_type=MESH
        )

    def tab_copy(k):
        here = tab_all.at[pl.ds(pl.multiple_of(t * owned, owned), owned)]
        return remote(tab, here, tab_ssem.at[k], tab_rsem.at[k], {"task": lax.rem(t + k, owners)})

    def x_copy(h, q):
        return remote(
            delta_ref.at[g, q], dbuf.at[t, g, q], x_ssem.at[h, q], x_rsem.at[h, q],
            {"task": lax.rem(t + 2 * h + 2, owners)},
        )

    def y_copy(h, q):
        src = lax.rem(t - 2 * h - 2 + owners, owners)
        return remote(
            dbuf.at[src, g, q], dbuf.at[src, g, q], y_ssem.at[h, q], y_rsem.at[h, q], {"groups": 1 - g}
        )

    def c_copy(h, q, half):
        src = lax.rem(t - 2 * h - 2 + owners, owners)
        slot = g if half == 0 else 1 - g
        return remote(
            dbuf.at[src, slot, q], dbuf.at[src, slot, q], c_ssem.at[half, h, q], c_rsem.at[half, h, q],
            {"task": twin},
        )

    for piece, ref in enumerate((row_ref, col_ref, live_ref)):
        for s in range(2):
            column = ref[:, s : s + 1].astype(jnp.float32)
            at = (2 * piece + s) * 128
            tab[:, at : at + 128] = jnp.broadcast_to(column, (owned, 128)).astype(jnp.bfloat16)

    own_copy = remote(delta_ref, dbuf.at[t], own_ssem, own_rsem, {"task": twin})
    for k in range(1, owners):
        tab_copy(k).start()
    for q in range(PIECES):
        for h in range(len(hops)):
            x_copy(h, q).start()
    own_copy.start()
    tab_all[pl.ds(pl.multiple_of(t * owned, owned), owned), :] = tab[...]

    def base_step(i, carry):
        @pl.when(i + RING - 1 < steps)
        def _():
            wcopy(i + RING - 1).start()

        wcopy(i).wait()
        got = jnp.dot(att_ref[...], wbuf[lax.rem(i, RING)], preferred_element_type=jnp.float32)
        for e in range(PAIR):
            part[step_at(i), e] = got[:, e * 128 : (e + 1) * 128]
        return carry

    def decoded(blocks, scale):
        whole = blocks.astype(jnp.int32).astype(jnp.float32).reshape(rows // 8, 8, 128)
        return (whole * scale[None]).reshape(rows, 128)

    def encode(total, ref, scales, at):
        cut = total.reshape(rows // 8, 8, 128)
        top = jnp.maximum(jnp.max(jnp.abs(cut), axis=0), 1e-30)
        scales[at] = top * (1.0 / LEVELS)
        levels = jnp.round(cut * (LEVELS / top)[None]).reshape(rows, 128)
        ref[at] = levels.astype(jnp.int32).astype(jnp.int16)

    def f_copies(i):
        where = {"tensor": z + 1}
        return (
            remote(fsend.at[i], frecv.at[i], f_ssem.at[i], f_rsem.at[i], where),
            remote(fscale.at[i], frscale.at[i], fs_ssem.at[i], fs_rsem.at[i], where),
        )

    def b_copies(i):
        where = {"tensor": z - 1}
        return (
            remote(bsend.at[i], brecv.at[i], b_ssem.at[i], b_rsem.at[i], where),
            remote(bscale.at[i], brscale.at[i], bs_ssem.at[i], bs_rsem.at[i], where),
        )

    def near_end(i, carry):
        @pl.when(z == 0)
        def _():
            for e in range(PAIR):
                encode(part[(n - 1 - i // per) * per + i % per, e], fsend, fscale, (i, e))
            for copy in f_copies(i):
                copy.start()

        @pl.when(z == n - 1)
        def _():
            for e in range(PAIR):
                encode(part[i, e], bsend, bscale, (i, e))
            for copy in b_copies(i):
                copy.start()

        return carry

    for q in range(PIECES):
        lax.fori_loop(steps * q // PIECES, steps * (q + 1) // PIECES, base_step, 0)
        if (q + 1) * n >= PIECES and q * n < PIECES:
            lax.fori_loop(0, per, near_end, 0)
        for h in range(len(hops)):
            x_copy(h, q).wait_recv()
            y_copy(h, q).start()
            c_copy(h, q, 0).start()

    lax.fori_loop(per, (n - 1) * per, near_end, 0)

    for k in range(1, owners):
        tab_copy(k).wait_recv()
    tasks = tab_all.shape[0]
    for i in range(rows // 128):
        line = jnp.broadcast_to(tag_ref[i : i + 1, :].astype(jnp.float32), (128, 128))
        tagf[i * 128 : (i + 1) * 128, :] = line.T
    hits = tagf[:, :tasks] == lax.broadcasted_iota(jnp.int32, (rows, tasks), 1).astype(jnp.float32)
    onehot = jnp.where(hits, 1.0, 0.0).astype(jnp.bfloat16)
    ctab[...] = tab_all[:, 256:512]
    onehot_info[...] = jnp.dot(onehot, tab_all[...], preferred_element_type=jnp.float32)
    tile = 64

    def choose(i, carry):
        at = pl.ds(pl.multiple_of(i * tile, tile), tile)
        heads = [onehot_info[at, s * 128 : (s + 1) * 128] for s in range(2)]
        picked = [jnp.zeros((tile, 128), jnp.float32) for s in range(2)]
        for h in range(att_ref.shape[1] // 128):
            block = att_ref[at, h * 128 : (h + 1) * 128].astype(jnp.float32)
            for s in range(2):
                picked[s] = jnp.where(heads[s] == float(h), block, picked[s])
        for s in range(2):
            chosen[s, at, :] = picked[s]
        return carry

    lax.fori_loop(0, rows // tile, choose, 0)
    vals[...] = jnp.zeros_like(vals)

    def add_half(ref, owner, half):
        each = owned // 2 // PIECES

        def body(q, carry):
            for s in range(2):
                for e in range(each):
                    task = owner * owned + half * (owned // 2) + q * each + e
                    spread[:, e * 128 : (e + 1) * 128] = jnp.where(
                        tagf[...] == task.astype(jnp.float32), chosen[s], 0.0
                    ).astype(jnp.bfloat16)
                source = ref[half, q, :, s].reshape(each * 128, 128)
                vals[s] += jnp.dot(spread[...], source, preferred_element_type=jnp.float32)
            return carry

        lax.fori_loop(0, PIECES, body, 0)

    for half in range(2):
        add_half(delta_ref, t, half)
    own_copy.wait_recv()
    for half in range(2):
        add_half(dbuf.at[twin], twin, half)
    for h in range(len(hops)):
        src = lax.rem(t - 2 * h - 2 + owners, owners)
        add_half(dbuf.at[src], src, g)
    for q in range(PIECES):
        for h in range(len(hops)):
            y_copy(h, q).wait_recv()
            c_copy(h, q, 1).start()
    for h in range(len(hops)):
        src = lax.rem(t - 2 * h - 2 + owners, owners)
        add_half(dbuf.at[src], src, 1 - g)
        other = lax.rem(twin - 2 * h - 2 + owners, owners)
        for q in range(PIECES):
            c_copy(h, q, 0).wait_recv()
            c_copy(h, q, 1).wait_recv()
        for half in range(2):
            add_half(dbuf.at[other], other, half)
    for s in range(2):
        vals[s] = vals[s] * onehot_info[:, (4 + s) * 128 : (5 + s) * 128]

    for s in range(2):
        encode(vals[s], vsend, vscale, s)

    def v_copies(k):
        where = {"tensor": lax.rem(z + k, n)}
        return (
            remote(vsend, vrecv.at[z], v_ssem.at[k], v_rsem.at[z], where),
            remote(vscale, vrscale.at[z], vs_ssem.at[k], vs_rsem.at[z], where),
            remote(ctab, ctab_in.at[z], ct_ssem.at[k], ct_rsem.at[z], where),
        )

    def v_arrivals(src):
        return (
            remote(vsend, vrecv.at[src], v_ssem.at[0], v_rsem.at[src], {"tensor": src}),
            remote(vscale, vrscale.at[src], vs_ssem.at[0], vs_rsem.at[src], {"tensor": src}),
            remote(ctab, ctab_in.at[src], ct_ssem.at[0], ct_rsem.at[src], {"tensor": src}),
        )

    for k in range(1, n):
        for copy in v_copies(k):
            copy.start()

    def block_sum(c, e):
        total = part[c, e]
        block = (c * PAIR + e).astype(jnp.float32)
        for s in range(2):
            mine = onehot_info[:, (2 + s) * 128 : (3 + s) * 128] == block
            total = total + jnp.where(mine, vals[s], 0.0)
        return total

    f_count = (n - 1 - z) * per
    b_count = z * per

    def chain(i, carry):
        @pl.when((i < f_count) & (z > 0))
        def _():
            at = (n - 1 - i // per) * per + i % per
            for copy in f_copies(i):
                copy.wait_recv()
            for e in range(PAIR):
                encode(part[at, e] + decoded(frecv[i, e], frscale[i, e]), fsend, fscale, (i, e))
            for copy in f_copies(i):
                copy.start()

        @pl.when((i < b_count) & (z < n - 1))
        def _():
            for copy in b_copies(i):
                copy.wait_recv()
            for e in range(PAIR):
                encode(part[i, e] + decoded(brecv[i, e], brscale[i, e]), bsend, bscale, (i, e))
            for copy in b_copies(i):
                copy.start()

        return carry

    lax.fori_loop(0, (n - 1) * per, chain, 0)

    for k in range(1, n):
        src = lax.rem(z + k, n)
        for copy in v_arrivals(src):
            copy.wait_recv()
        for s in range(2):
            far_vals[k - 1, s] = decoded(vrecv[src, s], vrscale[src, s])
        far_cols[k - 1] = jnp.dot(onehot, ctab_in[src], preferred_element_type=jnp.float32)

    def finish(j, carry):
        c = z * per + j
        for e in range(PAIR):
            part[c, e] = block_sum(c, e)

        for e in range(PAIR):
            block = (c * PAIR + e).astype(jnp.float32)
            for k in range(n - 1):
                for s in range(2):
                    there = far_cols[k, :, s * 128 : (s + 1) * 128] == block
                    part[c, e] += jnp.where(there, far_vals[k, s], 0.0)

        @pl.when(z < n - 1)
        def _():
            i = z * per + j
            for copy in b_copies(i):
                copy.wait_recv()
            for e in range(PAIR):
                part[c, e] += decoded(brecv[i, e], brscale[i, e])

        @pl.when(z > 0)
        def _():
            i = (n - 1 - z) * per + j
            for copy in f_copies(i):
                copy.wait_recv()
            for e in range(PAIR):
                part[c, e] += decoded(frecv[i, e], frscale[i, e])

        for e in range(PAIR):
            at = pl.ds(pl.multiple_of(j * WIDE + e * 128, 128), 128)
            out_ref[:, at] = part[c, e].astype(out_ref.dtype)
        return carry

    lax.fori_loop(0, per, finish, 0)

    def drain(i, carry):
        @pl.when(i < f_count)
        def _():
            for copy in f_copies(i):
                copy.wait_send()

        @pl.when(i < b_count)
        def _():
            for copy in b_copies(i):
                copy.wait_send()

        return carry

    lax.fori_loop(0, (n - 1) * per, drain, 0)
    for k in range(1, n):
        for copy in v_copies(k):
            copy.wait_send()

    for k in range(1, owners):
        tab_copy(k).wait_send()
    own_copy.wait_send()
    for q in range(PIECES):
        for h in range(len(hops)):
            x_copy(h, q).wait_send()
            y_copy(h, q).wait_send()
            c_copy(h, q, 0).wait_send()
            c_copy(h, q, 1).wait_send()


def local_fast(sizes, attention, out_weight, task_tags, delta_values, block_rows, block_columns, block_live):
    n, owners = sizes["tensor"], sizes["task"]
    rows = attention.shape[0]
    depth, width = out_weight.shape
    owned, slots, hd = delta_values.shape[:3]
    steps = width // WIDE
    chunk = width // n
    count = (n - 1) * (steps // n)
    tags = task_tags.reshape(rows // 128, 128)
    deltas = delta_values.reshape(2, PIECES, owned // (2 * PIECES), slots, hd, hd)
    vmem = pl.BlockSpec(memory_space=pltpu.VMEM)
    hop = max(owners // 2 - 1, 1)
    dma = pltpu.SemaphoreType.DMA
    sends = [
        pltpu.VMEM((count, PAIR, rows, 128), jnp.int16),
        pltpu.VMEM((count, PAIR, 8, 128), jnp.float32),
    ]
    return pl.pallas_call(
        functools.partial(kernel, n, owners),
        out_shape=jax.ShapeDtypeStruct((rows, chunk), jnp.bfloat16),
        in_specs=[vmem, pl.BlockSpec(memory_space=pl.ANY), vmem, vmem, vmem, vmem, vmem],
        out_specs=vmem,
        scratch_shapes=[
            pltpu.VMEM((steps, PAIR, rows, 128), jnp.float32),
            pltpu.VMEM((RING, depth, WIDE), jnp.bfloat16),
            pltpu.VMEM((rows, 128), jnp.float32),
            pltpu.VMEM((owned, 3 * slots * 128), jnp.bfloat16),
            pltpu.VMEM((owners * owned, 3 * slots * 128), jnp.bfloat16),
            pltpu.VMEM((owners * owned, slots * 128), jnp.bfloat16),
            pltpu.VMEM((n, owners * owned, slots * 128), jnp.bfloat16),
            pltpu.VMEM((rows, 3 * slots * 128), jnp.float32),
            pltpu.VMEM((slots, rows, 128), jnp.float32),
            pltpu.VMEM((slots, rows, 128), jnp.float32),
            pltpu.VMEM((owners, *deltas.shape), jnp.bfloat16),
            pltpu.VMEM((rows, owned // (2 * PIECES) * hd), jnp.bfloat16),
            pltpu.VMEM((slots, rows, 128), jnp.int16),
            pltpu.VMEM((slots, 8, 128), jnp.float32),
            pltpu.VMEM((n, slots, rows, 128), jnp.int16),
            pltpu.VMEM((n, slots, 8, 128), jnp.float32),
            pltpu.VMEM((n - 1, slots, rows, 128), jnp.float32),
            pltpu.VMEM((n - 1, rows, slots * 128), jnp.float32),
            *(sends * 4),
            dma((RING,)),
            dma((owners,)), dma((owners,)), dma, dma,
            dma((hop, PIECES)), dma((hop, PIECES)), dma((hop, PIECES)), dma((hop, PIECES)),
            dma((2, hop, PIECES)), dma((2, hop, PIECES)),
            *([dma((count,))] * 8),
            *([dma((n,))] * 6),
        ],
        compiler_params=pltpu.CompilerParams(
            collective_id=0, has_side_effects=True, vmem_limit_bytes=60 * 1024 * 1024
        ),
        cost_estimate=pl.CostEstimate(
            flops=2 * rows * depth * width, bytes_accessed=2 * depth * width, transcendentals=0
        ),
    )(attention, out_weight, tags, block_rows, block_columns, block_live, deltas)


def solution(mesh):
    in_specs = (
        P(("groups", "task"), "tensor"),
        P("tensor", None),
        P(("groups", "task")),
        P("task", "tensor", None, None),
        P("task", "tensor"),
        P("task", "tensor"),
        P("task", "tensor"),
    )
    out_specs = P(("groups", "task"), "tensor")
    fast = fits(mesh)
    local = functools.partial(local_fast, mesh.shape) if fast else local_general
    return jax.shard_map(local, mesh=mesh, in_specs=in_specs, out_specs=out_specs, check_vma=False)
```
